32 devices in a mesh: sky: 8 (over z, y), exp: 4 (over x, core).
Axes of the slice: x: 2, y: 2, z: 4, core: 2. Of those that a mesh axis runs over, the one named last changes fastest.
Arguments:
- sky_model: bfloat16 [2048, 1024], P('sky'), may hold values from -6 to 6
- exposure_data: bfloat16 [512, 128, 128], P(('sky', 'exp')), may hold values from -6 to 6
- pixel_mask: int32 [512, 128, 128], P(('sky', 'exp')), may hold values 0 or 1
- block_owner: int32 [512, 1], P(('sky', 'exp')), may hold values from 0 to 7; in each aligned block of 16 rows (0 to 15, 16 to 31, ...) at most 2 rows name the same one
- block_local: int32 [512], P(('sky', 'exp')), may hold values from 0 to 15
- psf_cell: int32 [512], P(('sky', 'exp')), may hold values from 0 to 15
- psf_table: bfloat16 [64, 1681], P('exp'), may hold values from -0.15625 to 0.15625
Outputs:
- model_grad: float32 [2048, 1024], P('sky', 'exp')
- residual: bfloat16 [512, 128, 128], P(('sky', 'exp'))
The draws below stay inside these ranges and needn't reach their ends.
Inputs may be any that keep to these rules, and one draw needn't show every extreme that they name: `block_owner`: among the pieces of one device no sky index is named more than 2 times.
All inputs are finite; a program needn't handle non-finite values. No bound on the sum of `pixel_mask` on one device may be relied on, other than what follows from the above.
Results may differ from the reference program's by a relative error of at most 0.014.
Values may be sent and summed in bfloat16 or wider, within the bound.
A program may use at most 64 MiB of HBM per device.

```python
import math
import jax
import jax.numpy as jnp
import numpy as np
from jax import lax

B = 128
PSF = 41
HALO = 20
CAP = 2
CELLS = 16
BR = 2
BC = 8
P_DEV = 16
NBD = 16
NY = 2048
NX = 1024
PIECES = 512
N_SKY = 8
N_EXP = 4


def set_ends(drawn, own_key, least, top_value):
    index_at = [jax.random.randint(jax.random.fold_in(own_key, axis), (), 0, length) for axis, length in enumerate(drawn.shape)]
    widest = drawn.shape.index(max(drawn.shape))
    neighbour = index_at[:widest] + [(index_at[widest] + 1) % drawn.shape[widest]] + index_at[widest + 1:]
    return drawn.at[tuple(index_at)].set(least).at[tuple(neighbour)].set(top_value)


def level_of(rng, shape, shards, least, largest):
    def one(position, blocks):
        draws = jax.random.uniform(jax.random.fold_in(jax.random.fold_in(rng, 6), position), (blocks,), jnp.float32, least / len(shards), largest / len(shards))
        return jnp.repeat(jnp.exp(draws), shape[position] // blocks).reshape((-1,) + (1,) * (len(shape) - position - 1))

    level = one(*shards[0])
    for cut in shards[1:]:
        level = level * one(*cut)
    return level


def routed_block(stream_key, own, number, rows, count, top, reach, skew):
    order = jax.random.permutation(stream_key, count)
    packed, usual = portions_of(count, rows * top, reach, skew, True), portions_of(count, rows * top, reach, skew, False)
    places = jnp.arange(count)

    def named(lengths, turn):
        used = int((lengths > 0).sum())
        fixed = max(1, used // 4)
        moved = fixed + (places - fixed + turn * (used - fixed)) % max(1, count - fixed)
        return jnp.zeros((count,), jnp.int32).at[order[jnp.where(places < fixed, places, moved)]].set(jnp.asarray(lengths, jnp.int32))

    lengths = jnp.where(number % 4 == 0, named(packed, number // 4), named(usual, number - number // 4 - 1))
    mixed = jax.random.permutation(jax.random.fold_in(own, 3), count)
    donor, receiver = mixed[0:count // 2 * 2:2], mixed[1:count // 2 * 2:2]
    slack = jnp.minimum(lengths[donor] - 1, reach - lengths[receiver]) // 2
    slack = jnp.where((donor == order[0]) | (receiver == order[0]) | (lengths[receiver] == 0), 0, jnp.maximum(slack, 0))
    moved = jax.random.randint(jax.random.fold_in(own, 4), (count // 2,), 0, 1 << 20) % (slack + 1)
    lengths = lengths.at[donor].add(-moved).at[receiver].add(moved)
    labels = jnp.searchsorted(jnp.cumsum(lengths), jnp.arange(rows * top), side="right").astype(jnp.int32)
    table = labels.reshape(top, rows).T
    table = table[jax.random.permutation(jax.random.fold_in(own, 1), rows)]
    turn = jax.random.randint(jax.random.fold_in(own, 2), (rows, 1), 0, top)
    return jnp.take_along_axis(table, (jnp.arange(top)[None, :] + turn) % top, axis=1)


def portions_of(amount, total, most, lean, full):
    loads = [(1 << 20) // math.isqrt(standing ** lean) + 1 for standing in range(1, amount + 1)]
    largest = most if full else min(most, max(-(-total // amount), total * loads[0] // sum(loads)))
    least = 1 if total - largest >= amount - 1 else 0
    given, rest = [largest] + [least] * (amount - 1), total - largest - least * (amount - 1)
    while rest > 0:
        free = [i for i in range(1, amount) if given[i] < largest] or [i for i in range(1, amount) if given[i] < most]
        pool, budget = sum([loads[i] for i in free]), rest
        for i in free:
            extra = min(most - given[i], max(1, budget * loads[i] // pool), rest)
            given[i] = given[i] + extra
            rest = rest - extra
    return np.array(given)


def scatter_about(stream_key, dims, scale, reach, pieces=(), held_as=jnp.bfloat16):
    result = jax.random.normal(stream_key, dims, jnp.float32) * scale
    if len(pieces) > 0:
        result = level_of(stream_key, dims, pieces, -0.22, 0.18) * result
    return jnp.clip(result, min=-reach, max=reach).astype(held_as)


def setup_inputs(seed: int = 0) -> dict:
    splits = jax.random.split(jax.random.key(seed), 8)
    sky_model = scatter_about(splits[0], (NY, NX), 1.0, 6.0, ((0, 8),))
    exposure_data = scatter_about(splits[1], (PIECES, B, B), 1.0, 6.0, ((0, 32),))
    pixel_mask = set_ends((jax.random.randint(splits[2], (PIECES, B, B), 0, 4) < 3).astype(jnp.int32), jax.random.fold_in(splits[2], 1), 0, 1)
    block_owner_keys = jax.random.split(jax.random.fold_in(splits[3], 1), PIECES // P_DEV)
    block_owner_turns = jax.random.permutation(jax.random.fold_in(splits[3], 3), PIECES // P_DEV)
    block_owner = jax.vmap(lambda own, number: routed_block(jax.random.fold_in(splits[3], 2), own, number, P_DEV, N_SKY, 1, CAP, 2))(block_owner_keys, block_owner_turns).reshape((PIECES, 1))
    block_local = set_ends(jax.random.randint(splits[4], (PIECES,), 0, NBD), jax.random.fold_in(splits[4], 1), 0, NBD - 1).astype(jnp.int32)
    psf_cell = set_ends(jax.random.randint(splits[5], (PIECES,), 0, CELLS), jax.random.fold_in(splits[5], 1), 0, CELLS - 1).astype(jnp.int32)
    psf_table = scatter_about(splits[6], (N_EXP * CELLS, PSF * PSF), (PSF * PSF) ** -0.5, 0.15625, ((0, 4),))
    return {"sky_model": sky_model, "exposure_data": exposure_data, "pixel_mask": pixel_mask, "block_owner": block_owner, "block_local": block_local, "psf_cell": psf_cell, "psf_table": psf_table}


def correlate(field, kernel, out_size):
    extent = field.shape[0]
    padded_kernel = jnp.zeros((extent, extent), field.dtype).at[:PSF, :PSF].set(kernel)
    spectrum = jnp.fft.rfft2(field) * jnp.conj(jnp.fft.rfft2(padded_kernel))
    return jnp.fft.irfft2(spectrum, s=(extent, extent))[:out_size, :out_size]


def reference(sky_model, exposure_data, pixel_mask, block_owner, block_local, psf_cell, psf_table):
    extent = B + 2 * HALO
    padded = jnp.pad(sky_model.astype(jnp.float32), HALO)
    piece_ids = jnp.arange(PIECES, dtype=jnp.int32)
    owner_exp = (piece_ids // P_DEV) % N_EXP
    row_start = ((block_owner[:, 0] * BR + block_local // BC) * B).astype(jnp.int32)
    col_start = ((block_local % BC) * B).astype(jnp.int32)
    kernel_row = (owner_exp * CELLS + psf_cell).astype(jnp.int32)

    def one_piece(canvas, item):
        row_first, col_first, kernel_index, observed, keep = item
        patch = lax.dynamic_slice(padded, (row_first, col_first), (extent, extent))
        kernel = psf_table[kernel_index].astype(jnp.float32).reshape(PSF, PSF)
        predicted = correlate(patch, kernel, B)
        residual = (keep.astype(jnp.float32) * (predicted - observed.astype(jnp.float32))).astype(jnp.bfloat16)
        widened = jnp.pad(residual.astype(jnp.float32), 2 * HALO)
        adjoint = correlate(widened, kernel[::-1, ::-1], extent)
        current = lax.dynamic_slice(canvas, (row_first, col_first), (extent, extent))
        canvas = lax.dynamic_update_slice(canvas, current + adjoint, (row_first, col_first))
        return canvas, residual

    start = jnp.zeros(padded.shape, jnp.float32)
    canvas, residuals = lax.scan(one_piece, start, (row_start, col_start, kernel_row, exposure_data, pixel_mask))
    return canvas[HALO:-HALO, HALO:-HALO], residuals
```

```python
import functools

import jax
import jax.numpy as jnp
from jax import lax
from jax.experimental import pallas as pl
from jax.experimental.pallas import tpu as pltpu
from jax.sharding import PartitionSpec as P

B = 128
PSF = 41
HALO = 20
CAP = 2
EXT = B + 2 * HALO
TAPS = 48
ROWPAD = 32
COLPAD = 128
AROWS = 176


def from_behind(x, axis, by):
    devices = lax.axis_size(axis)
    pairs = [(i, i + by) for i in range(devices) if 0 <= i + by < devices]
    return lax.ppermute(x, axis, pairs)


def fold_blocks(per_block, block_rows, per_row):
    extent = B + 2 * HALO
    margin = 2 * HALO
    grid = per_block.reshape(block_rows, per_row, extent, extent)
    col_main = grid[..., :B].transpose(0, 2, 1, 3).reshape(block_rows, extent, per_row * B)
    col_tail = jnp.pad(grid[..., B:], ((0, 0), (0, 0), (0, 0), (0, B - margin)))
    col_tail = col_tail.transpose(0, 2, 1, 3).reshape(block_rows, extent, per_row * B)
    width = per_row * B + margin
    columns = (
        jnp.pad(col_main, ((0, 0), (0, 0), (0, margin)))
        + jnp.pad(col_tail, ((0, 0), (0, 0), (B, 0)))[:, :, :width]
    )
    row_main = columns[:, :B].reshape(block_rows * B, width)
    row_tail = jnp.pad(columns[:, B:], ((0, 0), (0, B - margin), (0, 0))).reshape(
        block_rows * B, width
    )
    height = block_rows * B + margin
    return jnp.pad(row_main, ((0, margin), (0, 0))) + jnp.pad(row_tail, ((B, 0), (0, 0)))[:height]


def piece_kernel(row_ref, col_ref, cell_ref, slot_ref, whole, base, observed, keep,
                 residual_out, adjoint_out, tt, patch, rbuf):
    piece = pl.program_id(0)

    @pl.when(piece == 0)
    def _():
        tt[...] = jnp.zeros_like(tt)
        rbuf[...] = jnp.zeros_like(rbuf)

    lane = lax.broadcasted_iota(jnp.int32, (PSF, 16, 128), 2)
    taps = base[0].astype(jnp.float32)
    for step in range(B // 16):
        first = 16 * step
        turned = pltpu.roll(taps, first, 2) if first else taps
        over = first + 56 - 128
        if over > 0:
            low = jnp.where(lane >= first, turned, 0.0)
            high = jnp.where(lane < over, turned, 0.0)
            tt[0:PSF, first : first + 16, 128:256] = high.astype(jnp.bfloat16)
        else:
            low = turned
        tt[0:PSF, first : first + 16, 0:128] = low.astype(jnp.bfloat16)

    row0 = pl.multiple_of(row_ref[piece], 128)
    col0 = pl.multiple_of(col_ref[piece], 128)
    window = whole[pl.ds(row0, 192), pl.ds(col0, 384)].astype(jnp.float32)
    shifted = window[ROWPAD - HALO : ROWPAD - HALO + AROWS]
    shifted = pltpu.roll(shifted, 384 - (COLPAD - HALO), 1)[:, 0:256]
    patch[...] = shifted.astype(jnp.bfloat16)

    total = None
    for s in range(14, -1, -2):
        acc = None
        for q in range(3):
            a = 16 * q + s
            if a >= PSF:
                continue
            band = tt[a : a + 2].reshape(256, 256)
            term = lax.dot_general(patch[16 * q : 16 * q + 144, :], band,
                                   (((1,), (1,)), ((), ())), preferred_element_type=jnp.float32)
            acc = term if acc is None else acc + term
        if total is None:
            total = acc[:, 128:256]
        else:
            total = pltpu.roll(total, 143, 0) + acc[:, 128:256]
        total = pltpu.roll(total, 143, 0) + acc[:, 0:128]
    predicted = total[0:B]
    residual = (keep[0].astype(jnp.float32) * (predicted - observed[0].astype(jnp.float32)))
    residual = residual.astype(jnp.bfloat16)
    residual_out[0] = residual
    wide = jnp.concatenate([residual.astype(jnp.float32), jnp.zeros((16, B), jnp.float32)], 0)
    rbuf[32 : 32 + B, 0:128] = residual
    rbuf[32 : 32 + B + 16, 128:256] = pltpu.roll(wide, 1, 0).astype(jnp.bfloat16)

    back = None
    for s in range(14, -1, -2):
        acc = None
        for q in range(3):
            a = 16 * q + s
            if a >= PSF:
                continue
            band = tt[a : a + 2].reshape(256, 256)
            term = jnp.dot(rbuf[32 - 16 * q : 32 - 16 * q + AROWS, :], band,
                           preferred_element_type=jnp.float32)
            acc = term if acc is None else acc + term
        back = acc if back is None else pltpu.roll(back, 2, 0) + acc
    adjoint_out[0] = back.astype(jnp.bfloat16)


def run_pieces(rows, cols, cells, slots, whole, base, observed, keep, slot_total):
    count = observed.shape[0]
    flops = count * 21 * 2 * 256 * 256 * (144 + AROWS)
    return pl.pallas_call(
        piece_kernel,
        grid_spec=pltpu.PrefetchScalarGridSpec(
            num_scalar_prefetch=4,
            grid=(count,),
            in_specs=[
                pl.BlockSpec(whole.shape, lambda p, r, c, k, s: (0, 0)),
                pl.BlockSpec((1, PSF, 16, 128), lambda p, r, c, k, s: (k[p], 0, 0, 0)),
                pl.BlockSpec((1, B, B), lambda p, r, c, k, s: (p, 0, 0)),
                pl.BlockSpec((1, B, B), lambda p, r, c, k, s: (p, 0, 0)),
            ],
            out_specs=[
                pl.BlockSpec((1, B, B), lambda p, r, c, k, s: (p, 0, 0)),
                pl.BlockSpec((1, AROWS, 256), lambda p, r, c, k, s: (s[p], 0, 0)),
            ],
            scratch_shapes=[
                pltpu.VMEM((TAPS, B, 256), jnp.bfloat16),
                pltpu.VMEM((AROWS, 256), jnp.bfloat16),
                pltpu.VMEM((32 + AROWS, 256), jnp.bfloat16),
            ],
        ),
        out_shape=[
            jax.ShapeDtypeStruct((count, B, B), jnp.bfloat16),
            jax.ShapeDtypeStruct((slot_total, AROWS, 256), jnp.bfloat16),
        ],
        compiler_params=pltpu.CompilerParams(vmem_limit_bytes=56 * 2**20),
        cost_estimate=pl.CostEstimate(flops=flops, bytes_accessed=16 * 2**20, transcendentals=0),
        name="pieces",
    )(rows, cols, cells, slots, whole, base, observed, keep)


def shards(sky_model, exposure_data, pixel_mask, block_owner, block_local, psf_cell, psf_table):
    sky_count = lax.axis_size("sky")
    extent = EXT
    stripe_rows = sky_model.shape[0]
    stripe_cols = sky_model.shape[1]
    per_row = stripe_cols // B
    block_rows = stripe_rows // B
    block_total = block_rows * per_row
    piece_count = exposure_data.shape[0]
    slot_total = sky_count * CAP
    owner_sky = block_owner[:, 0]
    earlier = lax.broadcasted_iota(jnp.int32, (piece_count, piece_count), 1) < lax.broadcasted_iota(
        jnp.int32, (piece_count, piece_count), 0
    )
    same_owner = owner_sky[:, None] == owner_sky[None, :]
    rank_within = jnp.sum((same_owner & earlier).astype(jnp.int32), axis=1)
    slot_index = owner_sky * CAP + rank_within
    requests_flat = jnp.full((slot_total,), -1, jnp.int32).at[slot_index].set(block_local)
    requests = requests_flat.reshape(sky_count, CAP)
    cell_count = psf_table.shape[0]
    kernels = psf_table.reshape(cell_count, PSF, PSF)
    base = jnp.stack(
        [jnp.pad(kernels, ((0, 0), (0, 0), (j, 128 - PSF - j))) for j in range(16)], axis=2
    )

    whole = lax.all_gather(sky_model, "sky", axis=0, tiled=True)
    padded = jnp.pad(whole, ((ROWPAD, ROWPAD), (COLPAD, COLPAD)))
    row_start = (owner_sky * block_rows + block_local // per_row) * B
    col_start = block_local % per_row * B
    residuals, adjoints = run_pieces(
        row_start, col_start, psf_cell, slot_index, padded, base, exposure_data, pixel_mask, slot_total
    )
    outgoing = jnp.where((requests_flat >= 0)[:, None, None], adjoints, 0)[:, :extent, :extent]
    outgoing = outgoing.reshape(sky_count, CAP, extent, extent)
    received, received_ids = (
        lax.all_to_all(outgoing, "sky", split_axis=0, concat_axis=0, tiled=True).astype(jnp.float32),
        lax.all_to_all(requests, "sky", split_axis=0, concat_axis=0, tiled=True),
    )
    contributions = received.reshape(slot_total, extent, extent)
    asked_ids = received_ids.reshape(slot_total)
    selector = (asked_ids[:, None] == lax.broadcasted_iota(jnp.int32, (1, block_total), 1)).astype(
        jnp.float32
    )
    per_block = jnp.einsum("nl,nuv->luv", selector, contributions, precision=lax.Precision.HIGHEST)
    canvas = fold_blocks(per_block, block_rows, per_row)
    core = canvas[:, HALO : HALO + stripe_cols]
    from_below = from_behind(core[:HALO].astype(jnp.bfloat16), "sky", -1).astype(jnp.float32)
    from_above = from_behind(core[stripe_rows + HALO :].astype(jnp.bfloat16), "sky", 1).astype(
        jnp.float32
    )
    middle = core[HALO : stripe_rows + HALO]
    folded = (
        middle
        + jnp.pad(from_above, ((0, stripe_rows - HALO), (0, 0)))
        + jnp.pad(from_below, ((stripe_rows - HALO, 0), (0, 0)))
    )
    gradient = lax.psum_scatter(
        folded.astype(jnp.bfloat16), "exp", scatter_dimension=1, tiled=True
    ).astype(jnp.float32)
    return (gradient, residuals)


def solution(mesh):
    in_specs = (
        P("sky", None),
        P(("sky", "exp"), None, None),
        P(("sky", "exp"), None, None),
        P(("sky", "exp"), None),
        P(("sky", "exp")),
        P(("sky", "exp")),
        P("exp", None),
    )
    out_specs = (P("sky", "exp"), P(("sky", "exp"), None, None))
    return jax.shard_map(shards, mesh=mesh, in_specs=in_specs, out_specs=out_specs, check_vma=False)
```

```python
import functools

import jax
import jax.numpy as jnp
from jax import lax
from jax.experimental import pallas as pl
from jax.experimental.pallas import tpu as pltpu
from jax.sharding import PartitionSpec as P

B = 128
PSF = 41
HALO = 20
CAP = 2
EXT = B + 2 * HALO
TAPS = 48
ROWPAD = 32
COLPAD = 128
AROWS = 176


MESH = pl.DeviceIdType.MESH
PACKED = 224
FOLD = 56
RIM = 32


def ring_place(sky, count):
    odd = sky % 2
    return (sky // 2) * (1 - odd) + (count - 1 - sky // 2) * odd


def ring_sky(place, count):
    late = place // (count // 2)
    return 2 * place * (1 - late) + (2 * (count - 1 - place) + 1) * late


def gather_kernel(count, cuts, stripe, whole, zero, ring_send, ring_recv, pair_send, pair_recv, local_sem):
    sky = lax.axis_index("sky")
    own = lax.axis_index("exp")
    core = own % 2
    pair = own + 1 - 2 * core
    place = ring_place(sky, count)
    ahead = ring_sky((place + 1) % count, count)
    behind = ring_sky((place + count - 1) % count, count)
    rows, cols = stripe.shape
    part = rows // (4 * cuts)

    barrier = pltpu.get_barrier_semaphore()
    for target in ((ahead, own), (behind, own), (sky, pair)):
        pl.semaphore_signal(barrier, inc=1, device_id=target, device_id_type=MESH)
    pl.semaphore_wait(barrier, 3)

    def inner(way, cut):
        return core * (rows // 2) + way * (rows // 4) + cut * part

    def spot(origin, way, cut):
        first = pl.multiple_of(ROWPAD + origin * rows + inner(way, cut), 16)
        return whole.at[pl.ds(first, part), pl.ds(COLPAD, cols)]

    def ring_copy(step, way, cut):
        sign = 1 - 2 * way
        origin = ring_sky((place + count - sign * step) % count, count)
        if step == 0:
            block = stripe.at[pl.ds(pl.multiple_of(inner(way, cut), 16), part), :]
        else:
            block = spot(origin, way, cut)
        return pltpu.make_async_remote_copy(
            src_ref=block, dst_ref=spot(origin, way, cut),
            send_sem=ring_send.at[step, way, cut], recv_sem=ring_recv.at[step, way, cut],
            device_id=((behind if way else ahead), own), device_id_type=MESH)

    def pair_copy(step, way, cut):
        sign = 1 - 2 * way
        origin = ring_sky((place + count - sign * step) % count, count)
        return pltpu.make_async_remote_copy(
            src_ref=spot(origin, way, cut), dst_ref=spot(origin, way, cut),
            send_sem=pair_send.at[step - 1, way, cut], recv_sem=pair_recv.at[step - 1, way, cut],
            device_id=(sky, pair), device_id_type=MESH)

    sends, pairs = {}, []
    for cut in range(cuts):
        for way in range(2):
            sends[0, way, cut] = ring_copy(0, way, cut)
            sends[0, way, cut].start()

    zero[...] = jnp.zeros_like(zero)
    total = whole.shape[0]
    fills = []
    mine = pl.multiple_of(ROWPAD + sky * rows, 16)
    fills.append(pltpu.make_async_copy(stripe, whole.at[pl.ds(mine, rows), pl.ds(COLPAD, cols)], local_sem.at[0]))
    for side in range(2):
        fills.append(pltpu.make_async_copy(
            zero, whole.at[:, pl.ds(side * (COLPAD + cols), COLPAD)], local_sem.at[1 + side]))
    for side in range(2):
        for block in range(cols // COLPAD):
            fills.append(pltpu.make_async_copy(
                zero.at[pl.ds(0, ROWPAD), :],
                whole.at[pl.ds(side * (total - ROWPAD), ROWPAD), pl.ds(COLPAD * (1 + block), COLPAD)],
                local_sem.at[3 + side * (cols // COLPAD) + block]))
    for fill in fills:
        fill.start()

    for step in range(1, count):
        for cut in range(cuts):
            for way in range(2):
                sends[step - 1, way, cut].wait_recv()
                if step < count - 1:
                    sends[step, way, cut] = ring_copy(step, way, cut)
                    sends[step, way, cut].start()
                extra = pair_copy(step, way, cut)
                extra.start()
                pairs.append((step, way, cut, extra))
    for copy in sends.values():
        copy.wait_send()
    for step, way, cut, extra in pairs:
        extra.wait_send()
        extra.wait_recv()
    for fill in fills:
        fill.wait()


def gather_model(stripe):
    count = lax.axis_size("sky")
    rows, cols = stripe.shape
    cuts = 2
    shape = (count * rows + 2 * ROWPAD, cols + 2 * COLPAD)
    steps = (count - 1, 2, cuts)
    return pl.pallas_call(
        functools.partial(gather_kernel, count, cuts),
        out_shape=jax.ShapeDtypeStruct(shape, stripe.dtype),
        in_specs=[pl.BlockSpec(memory_space=pl.ANY)],
        out_specs=pl.BlockSpec(memory_space=pl.ANY),
        scratch_shapes=[
            pltpu.VMEM((shape[0], COLPAD), stripe.dtype),
            pltpu.SemaphoreType.DMA(steps),
            pltpu.SemaphoreType.DMA(steps),
            pltpu.SemaphoreType.DMA(steps),
            pltpu.SemaphoreType.DMA(steps),
            pltpu.SemaphoreType.DMA((3 + 2 * (cols // COLPAD),)),
        ],
        compiler_params=pltpu.CompilerParams(
            collective_id=0, has_side_effects=True, vmem_limit_bytes=32 * 2**20),
        name="gather_model",
    )(stripe)


def exchange_kernel(count, data, asked, got, got_asked, data_send, data_recv, id_send, id_recv, local_sem):
    sky = lax.axis_index("sky")
    own = lax.axis_index("exp")
    barrier = pltpu.get_barrier_semaphore()
    for turn in range(1, count):
        pl.semaphore_signal(barrier, inc=1, device_id=((sky + turn) % count, own), device_id_type=MESH)
    pl.semaphore_wait(barrier, count - 1)
    copies = []
    for turn in range(1, count):
        target = (sky + turn) % count
        for source, dest, send, recv in ((data, got, data_send, data_recv), (asked, got_asked, id_send, id_recv)):
            copy = pltpu.make_async_remote_copy(
                src_ref=source.at[target], dst_ref=dest.at[sky],
                send_sem=send.at[turn - 1], recv_sem=recv.at[turn - 1],
                device_id=(target, own), device_id_type=MESH)
            copy.start()
            copies.append(copy)
    for place, (source, dest) in enumerate(((data, got), (asked, got_asked))):
        copy = pltpu.make_async_copy(source.at[sky], dest.at[sky], local_sem.at[place])
        copy.start()
        copies.append(copy)
    for copy in copies:
        copy.wait()


def exchange(data, asked):
    count = lax.axis_size("sky")
    return pl.pallas_call(
        functools.partial(exchange_kernel, count),
        out_shape=[jax.ShapeDtypeStruct(x.shape, x.dtype) for x in (data, asked)],
        in_specs=[pl.BlockSpec(memory_space=pl.ANY)] * 2,
        out_specs=[pl.BlockSpec(memory_space=pl.ANY)] * 2,
        scratch_shapes=[pltpu.SemaphoreType.DMA((count - 1,))] * 4 + [pltpu.SemaphoreType.DMA((2,))],
        compiler_params=pltpu.CompilerParams(
            collective_id=1, has_side_effects=True, vmem_limit_bytes=32 * 2**20),
        name="exchange",
    )(data, asked)


def fold_kernel(stripe_rows, stripe_cols, exps, ids, parts, out, canvas):
    per_row = stripe_cols // B
    canvas[...] = jnp.zeros_like(canvas)
    lane = lax.broadcasted_iota(jnp.int32, (FOLD, B), 1)

    def add(slot, carry):
        block = ids[slot]

        @pl.when(block >= 0)
        def _():
            row0 = pl.multiple_of(block // per_row * B, B)
            col0 = pl.multiple_of(block % per_row * B, B)
            values = parts[slot].astype(jnp.float32)
            canvas[pl.ds(row0, EXT), pl.ds(col0, B)] += values[0:EXT]
            tails = values[EXT:PACKED]
            for third in range(3):
                turned = pltpu.roll(tails, B - 2 * HALO * third, 1) if third else tails
                turned = jnp.where(lane < 2 * HALO, turned, 0.0)
                first = pl.multiple_of(row0 + FOLD * third, 8)
                canvas[pl.ds(first, FOLD), pl.ds(pl.multiple_of(col0 + B, B), B)] += turned

        return carry

    lax.fori_loop(0, ids.shape[0], add, 0)
    width = stripe_cols + B
    middle = pltpu.roll(canvas[...], width - HALO, 1)[:, 0:stripe_cols]
    upper = jnp.concatenate([jnp.zeros((RIM - HALO, stripe_cols), jnp.float32), middle[0:HALO]], 0)
    lower = middle[stripe_rows + HALO : stripe_rows + HALO + RIM]
    rows = jnp.concatenate([middle[HALO : HALO + stripe_rows], upper, lower], 0).astype(out.dtype)
    share = stripe_cols // exps
    for e in range(exps):
        out[e] = rows[:, e * share : (e + 1) * share]


def fold(ids, parts, stripe_rows, stripe_cols, exps):
    shape = (exps, stripe_rows + 2 * RIM, stripe_cols // exps)
    return pl.pallas_call(
        functools.partial(fold_kernel, stripe_rows, stripe_cols, exps),
        grid_spec=pltpu.PrefetchScalarGridSpec(
            num_scalar_prefetch=1,
            grid=(1,),
            in_specs=[pl.BlockSpec(parts.shape, lambda i, ids: (0, 0, 0))],
            out_specs=pl.BlockSpec(shape, lambda i, ids: (0, 0, 0)),
            scratch_shapes=[pltpu.VMEM((stripe_rows + 56, stripe_cols + B), jnp.float32)],
        ),
        out_shape=jax.ShapeDtypeStruct(shape, jnp.bfloat16),
        compiler_params=pltpu.CompilerParams(vmem_limit_bytes=40 * 2**20),
        name="fold",
    )(ids, parts)


def reduce_kernel(skies, exps, parts, out, held, rims, rims_in, send, recv, rim_send, rim_recv):
    sky = lax.axis_index("sky")
    own = lax.axis_index("exp")
    above, below = (sky + skies - 1) % skies, (sky + 1) % skies
    rows = out.shape[0]
    barrier = pltpu.get_barrier_semaphore()
    targets = [(sky, (own + turn) % exps) for turn in range(1, exps)] + [(above, own), (below, own)]
    for target in targets:
        pl.semaphore_signal(barrier, inc=1, device_id=target, device_id_type=MESH)
    pl.semaphore_wait(barrier, len(targets))
    copies = []
    for turn in range(1, exps):
        target = (own + turn) % exps
        copy = pltpu.make_async_remote_copy(
            src_ref=parts.at[target], dst_ref=held.at[turn - 1],
            send_sem=send.at[turn - 1], recv_sem=recv.at[turn - 1],
            device_id=(sky, target), device_id_type=MESH)
        copy.start()
        copies.append(copy)
    for copy in copies:
        copy.wait_recv()

    def total(first, size):
        value = parts[own, first : first + size].astype(jnp.float32)
        for turn in range(1, exps):
            value = value + held[turn - 1, first : first + size].astype(jnp.float32)
        return value

    rims[0] = total(rows, RIM).astype(rims.dtype)
    rims[1] = total(rows + RIM, RIM).astype(rims.dtype)
    for side, target in enumerate((above, below)):
        copy = pltpu.make_async_remote_copy(
            src_ref=rims.at[side], dst_ref=rims_in.at[side],
            send_sem=rim_send.at[side], recv_sem=rim_recv.at[side],
            device_id=(target, own), device_id_type=MESH)
        copy.start()
        copies.append(copy)
    out[RIM : rows - RIM] = total(RIM, rows - 2 * RIM)
    top = total(0, RIM)
    bottom = total(rows - RIM, RIM)
    for copy in copies[-2:]:
        copy.wait_recv()
    has_above = jnp.full(top.shape, sky, jnp.int32) > 0
    has_below = jnp.full(top.shape, sky, jnp.int32) < skies - 1
    out[0:RIM] = top + jnp.where(has_above, rims_in[1].astype(jnp.float32), 0.0)
    out[rows - RIM : rows] = bottom + jnp.where(has_below, rims_in[0].astype(jnp.float32), 0.0)
    for copy in copies:
        copy.wait_send()


def reduce_parts(parts):
    skies, exps = lax.axis_size("sky"), lax.axis_size("exp")
    _, height, share = parts.shape
    rim = (2, RIM, share)
    return pl.pallas_call(
        functools.partial(reduce_kernel, skies, exps),
        out_shape=jax.ShapeDtypeStruct((height - 2 * RIM, share), jnp.float32),
        in_specs=[pl.BlockSpec(memory_space=pltpu.VMEM)],
        out_specs=pl.BlockSpec(memory_space=pltpu.VMEM),
        scratch_shapes=[
            pltpu.VMEM((exps - 1, height, share), parts.dtype),
            pltpu.VMEM(rim, parts.dtype),
            pltpu.VMEM(rim, parts.dtype),
            pltpu.SemaphoreType.DMA((exps - 1,)),
            pltpu.SemaphoreType.DMA((exps - 1,)),
            pltpu.SemaphoreType.DMA((2,)),
            pltpu.SemaphoreType.DMA((2,)),
        ],
        compiler_params=pltpu.CompilerParams(
            collective_id=2, has_side_effects=True, vmem_limit_bytes=32 * 2**20),
        name="reduce_parts",
    )(parts)


def piece_kernel(row_ref, col_ref, cell_ref, slot_ref, whole, base, observed, keep,
                 residual_out, adjoint_out, tt, patch, rbuf, spaced):
    piece = pl.program_id(0)

    @pl.when(piece == 0)
    def _():
        tt[...] = jnp.zeros_like(tt)
        rbuf[...] = jnp.zeros_like(rbuf)

    lane = lax.broadcasted_iota(jnp.int32, (PSF, 16, 128), 2)
    kernel = base[0].astype(jnp.float32)
    for j in range(16):
        spaced[pl.ds(j, TAPS, stride=16), :] = pltpu.roll(kernel, j, 1) if j else kernel
    taps = spaced[0 : PSF * 16].reshape(PSF, 16, 128)
    for step in range(B // 16):
        first = 16 * step
        turned = pltpu.roll(taps, first, 2) if first else taps
        over = first + 56 - 128
        if over > 0:
            low = jnp.where(lane >= first, turned, 0.0)
            high = jnp.where(lane < over, turned, 0.0)
            tt[0:PSF, first : first + 16, 128:256] = high.astype(jnp.bfloat16)
        else:
            low = turned
        tt[0:PSF, first : first + 16, 0:128] = low.astype(jnp.bfloat16)

    row0 = pl.multiple_of(row_ref[piece], 128)
    col0 = pl.multiple_of(col_ref[piece], 128)
    window = whole[pl.ds(row0, 192), pl.ds(col0, 384)].astype(jnp.float32)
    shifted = window[ROWPAD - HALO : ROWPAD - HALO + AROWS]
    shifted = pltpu.roll(shifted, 384 - (COLPAD - HALO), 1)[:, 0:256]
    patch[...] = shifted.astype(jnp.bfloat16)

    total = None
    for s in range(14, -1, -2):
        acc = None
        for q in range(3):
            a = 16 * q + s
            if a >= PSF:
                continue
            band = tt[a : a + 2].reshape(256, 256)
            term = lax.dot_general(patch[16 * q : 16 * q + 144, :], band,
                                   (((1,), (1,)), ((), ())), preferred_element_type=jnp.float32)
            acc = term if acc is None else acc + term
        if total is None:
            total = acc[:, 128:256]
        else:
            total = pltpu.roll(total, 143, 0) + acc[:, 128:256]
        total = pltpu.roll(total, 143, 0) + acc[:, 0:128]
    predicted = total[0:B]
    residual = (keep[0].astype(jnp.float32) * (predicted - observed[0].astype(jnp.float32)))
    residual = residual.astype(jnp.bfloat16)
    residual_out[0] = residual
    wide = jnp.concatenate([residual.astype(jnp.float32), jnp.zeros((16, B), jnp.float32)], 0)
    rbuf[32 : 32 + B, 0:128] = residual
    rbuf[32 : 32 + B + 16, 128:256] = pltpu.roll(wide, 1, 0).astype(jnp.bfloat16)

    back = None
    for s in range(14, -1, -2):
        acc = None
        for q in range(3):
            a = 16 * q + s
            if a >= PSF:
                continue
            band = tt[a : a + 2].reshape(256, 256)
            term = jnp.dot(rbuf[32 - 16 * q : 32 - 16 * q + AROWS, :], band,
                           preferred_element_type=jnp.float32)
            acc = term if acc is None else acc + term
        back = acc if back is None else pltpu.roll(back, 2, 0) + acc
    tails = back[0:EXT, 128:256]
    packed = tails[0:FOLD]
    for third in range(1, 3):
        packed = packed + pltpu.roll(tails[third * FOLD : (third + 1) * FOLD], 2 * HALO * third, 1)
    adjoint_out[0] = jnp.concatenate([back[0:EXT, 0:128], packed], 0).astype(jnp.bfloat16)


def run_pieces(rows, cols, cells, slots, whole, base, observed, keep, slot_total):
    count = observed.shape[0]
    flops = count * 21 * 2 * 256 * 256 * (144 + AROWS)
    return pl.pallas_call(
        piece_kernel,
        grid_spec=pltpu.PrefetchScalarGridSpec(
            num_scalar_prefetch=4,
            grid=(count,),
            in_specs=[
                pl.BlockSpec(whole.shape, lambda p, r, c, k, s: (0, 0)),
                pl.BlockSpec((1, TAPS, 128), lambda p, r, c, k, s: (k[p], 0, 0)),
                pl.BlockSpec((1, B, B), lambda p, r, c, k, s: (p, 0, 0)),
                pl.BlockSpec((1, B, B), lambda p, r, c, k, s: (p, 0, 0)),
            ],
            out_specs=[
                pl.BlockSpec((1, B, B), lambda p, r, c, k, s: (p, 0, 0)),
                pl.BlockSpec((1, PACKED, B), lambda p, r, c, k, s: (s[p], 0, 0)),
            ],
            scratch_shapes=[
                pltpu.VMEM((TAPS, B, 256), jnp.bfloat16),
                pltpu.VMEM((AROWS, 256), jnp.bfloat16),
                pltpu.VMEM((32 + AROWS, 256), jnp.bfloat16),
                pltpu.VMEM((TAPS * 16, 128), jnp.float32),
            ],
        ),
        out_shape=[
            jax.ShapeDtypeStruct((count, B, B), jnp.bfloat16),
            jax.ShapeDtypeStruct((slot_total, PACKED, B), jnp.bfloat16),
        ],
        compiler_params=pltpu.CompilerParams(vmem_limit_bytes=56 * 2**20),
        cost_estimate=pl.CostEstimate(flops=flops, bytes_accessed=16 * 2**20, transcendentals=0),
        name="pieces",
    )(rows, cols, cells, slots, whole, base, observed, keep)


def shards(sky_model, exposure_data, pixel_mask, block_owner, block_local, psf_cell, psf_table):
    sky_count = lax.axis_size("sky")
    exp_count = lax.axis_size("exp")
    stripe_rows, stripe_cols = sky_model.shape
    per_row = stripe_cols // B
    block_rows = stripe_rows // B
    piece_count = exposure_data.shape[0]
    slot_total = sky_count * CAP
    owner_sky = block_owner[:, 0]
    index = lax.broadcasted_iota(jnp.int32, (piece_count, piece_count), 0)
    earlier = lax.broadcasted_iota(jnp.int32, (piece_count, piece_count), 1) < index
    same_owner = owner_sky[:, None] == owner_sky[None, :]
    rank_within = jnp.sum((same_owner & earlier).astype(jnp.int32), axis=1)
    slot_index = owner_sky * CAP + rank_within
    named = slot_index[None, :] == lax.broadcasted_iota(jnp.int32, (slot_total, piece_count), 0)
    requests = jnp.sum(jnp.where(named, block_local[None, :] + 1, 0), axis=1) - 1
    requests = requests.reshape(sky_count, 1, CAP)
    requests = jnp.pad(requests, ((0, 0), (0, 7), (0, 128 - CAP)))
    cell_count = psf_table.shape[0]
    kernels = psf_table.reshape(cell_count, PSF, PSF)
    kernels = jnp.pad(kernels, ((0, 0), (0, TAPS - PSF), (0, 128 - PSF)))

    whole = gather_model(sky_model)
    row_start = (owner_sky * block_rows + block_local // per_row) * B
    col_start = block_local % per_row * B
    residuals, adjoints = run_pieces(
        row_start, col_start, psf_cell, slot_index, whole, kernels, exposure_data, pixel_mask, slot_total
    )
    received, asked = exchange(adjoints.reshape(sky_count, CAP, PACKED, B), requests)
    ids = asked[:, 0, :CAP].reshape(slot_total)
    parts = fold(ids, received.reshape(slot_total, PACKED, B), stripe_rows, stripe_cols, exp_count)
    return (reduce_parts(parts), residuals)


def solution(mesh):
    in_specs = (
        P("sky", None),
        P(("sky", "exp"), None, None),
        P(("sky", "exp"), None, None),
        P(("sky", "exp"), None),
        P(("sky", "exp")),
        P(("sky", "exp")),
        P("exp", None),
    )
    out_specs = (P("sky", "exp"), P(("sky", "exp"), None, None))
    return jax.shard_map(shards, mesh=mesh, in_specs=in_specs, out_specs=out_specs, check_vma=False)
```

```python
import functools

import jax
import jax.numpy as jnp
from jax import lax
from jax.experimental import pallas as pl
from jax.experimental.pallas import tpu as pltpu
from jax.sharding import PartitionSpec as P

B = 128
PSF = 41
HALO = 20
CAP = 2
EXT = B + 2 * HALO
TAPS = 48
ROWPAD = 32
COLPAD = 128
AROWS = 176


MESH = pl.DeviceIdType.MESH
PACKED = 224
FOLD = 56
RIM = 32


def ring_place(sky, count):
    odd = sky % 2
    return (sky // 2) * (1 - odd) + (count - 1 - sky // 2) * odd


def ring_sky(place, count):
    late = place // (count // 2)
    return 2 * place * (1 - late) + (2 * (count - 1 - place) + 1) * late


def gather_kernel(count, cuts, stripe, kernels, whole, table, zero, spaced, bands, ring_send, ring_recv,
                  pair_send, pair_recv, cross_send, cross_recv, last_send, last_recv, local_sem, table_sem):
    sky = lax.axis_index("sky")
    own = lax.axis_index("exp")
    core = own % 2
    half = (own % 4) // 2
    pair = own + 1 - 2 * core
    cross = own + 2 - 4 * half
    place = ring_place(sky, count)
    ahead = ring_sky((place + 1) % count, count)
    behind = ring_sky((place + count - 1) % count, count)
    rows, cols = stripe.shape
    cells = kernels.shape[0]
    part = rows // (8 * cuts)
    quarter, other = core + 2 * half, core + 2 * (1 - half)

    barrier = pltpu.get_barrier_semaphore()
    for target in ((ahead, own), (behind, own), (sky, pair), (sky, cross)):
        pl.semaphore_signal(barrier, inc=1, device_id=target, device_id_type=MESH)
    pl.semaphore_wait(barrier, 4)

    def inner(share, way, cut):
        return share * (rows // 4) + way * (rows // 8) + cut * part

    def spot(share, step, way, cut):
        origin = ring_sky((place + count - (1 - 2 * way) * step) % count, count)
        first = pl.multiple_of(ROWPAD + origin * rows + inner(share, way, cut), 16)
        return whole.at[pl.ds(first, part), pl.ds(COLPAD, cols)]

    def ring_copy(step, way, cut, first=False):
        dest = spot(quarter, step, way, cut)
        source = stripe.at[pl.ds(pl.multiple_of(inner(quarter, way, cut), 16), part), :] if first else dest
        return pltpu.make_async_remote_copy(
            src_ref=source, dst_ref=dest,
            send_sem=ring_send.at[step, way, cut], recv_sem=ring_recv.at[step, way, cut],
            device_id=((behind if way else ahead), own), device_id_type=MESH)

    def hand_on(share, step, way, cut, send, recv, target):
        block = spot(share, step, way, cut)
        return pltpu.make_async_remote_copy(
            src_ref=block, dst_ref=block, send_sem=send.at[step - 1, way, cut],
            recv_sem=recv.at[step - 1, way, cut], device_id=(sky, target), device_id_type=MESH)

    def pair_copy(step, way, cut):
        return hand_on(quarter, step, way, cut, pair_send, pair_recv, pair)

    def cross_copy(step, way, cut):
        return hand_on(quarter, step, way, cut, cross_send, cross_recv, cross)

    def last_copy(step, way, cut):
        return hand_on(other, step, way, cut, last_send, last_recv, pair)

    each = [(cut, way) for cut in range(cuts) for way in range(2)]
    for cut, way in each:
        ring_copy(0, way, cut, True).start()

    zero[...] = jnp.zeros_like(zero)
    total = whole.shape[0]
    fills = []
    mine = pl.multiple_of(ROWPAD + sky * rows, 16)
    fills.append(pltpu.make_async_copy(stripe, whole.at[pl.ds(mine, rows), pl.ds(COLPAD, cols)], local_sem.at[0]))
    for side in range(2):
        fills.append(pltpu.make_async_copy(
            zero, whole.at[:, pl.ds(side * (COLPAD + cols), COLPAD)], local_sem.at[1 + side]))
    for side in range(2):
        for block in range(cols // COLPAD):
            fills.append(pltpu.make_async_copy(
                zero.at[pl.ds(0, ROWPAD), :],
                whole.at[pl.ds(side * (total - ROWPAD), ROWPAD), pl.ds(COLPAD * (1 + block), COLPAD)],
                local_sem.at[3 + side * (cols // COLPAD) + block]))
    for fill in fills:
        fill.start()

    for slot in range(2):
        bands[slot, PSF] = jnp.zeros((B, 256), bands.dtype)
        bands[slot, 0:PSF, :, 128:256] = jnp.zeros((PSF, B, 128), bands.dtype)

    def table_copy(cell, slot):
        return pltpu.make_async_copy(bands.at[slot], table.at[cell], table_sem.at[slot])

    def build(cell):
        slot = cell % 2

        @pl.when(cell >= 2)
        def _():
            table_copy(cell, slot).wait()

        kernel = kernels[cell].astype(jnp.float32)
        for j in range(16):
            spaced[pl.ds(j, TAPS, stride=16), :] = pltpu.roll(kernel, j, 1) if j else kernel
        taps = spaced[0 : PSF * 16].reshape(PSF, 16, 128)
        lane = lax.broadcasted_iota(jnp.int32, (PSF, 16, 128), 2)
        for step in range(B // 16):
            first = 16 * step
            turned = pltpu.roll(taps, first, 2) if first else taps
            over = first + 56 - 128
            if over > 0:
                low = jnp.where(lane >= first, turned, 0.0)
                high = jnp.where(lane < over, turned, 0.0)
                bands[slot, 0:PSF, first : first + 16, 128:256] = high.astype(jnp.bfloat16)
            else:
                low = turned
            bands[slot, 0:PSF, first : first + 16, 0:128] = low.astype(jnp.bfloat16)
        table_copy(cell, slot).start()

    early = max(0, cells - (count - 1) * cuts)

    def build_early(cell, carry):
        build(cell)
        return carry

    lax.fori_loop(0, early, build_early, 0)

    def ring_step(step, carry):
        for cut in range(cuts):
            for way in range(2):
                ring_copy(step - 1, way, cut).wait_recv()

                @pl.when(step < count - 1)
                def _():
                    ring_copy(step, way, cut).start()

                cross_copy(step, way, cut).start()
                pair_copy(step, way, cut).start()

                @pl.when(step > 1)
                def _():
                    cross_copy(step - 1, way, cut).wait_recv()
                    last_copy(step - 1, way, cut).start()

            cell = early + (step - 1) * cuts + cut

            @pl.when(cell < cells)
            def _():
                build(cell)

        return carry

    lax.fori_loop(1, count, ring_step, 0)
    for cut, way in each:
        cross_copy(count - 1, way, cut).wait_recv()
        last_copy(count - 1, way, cut).start()

    def drain(step, carry):
        for cut, way in each:
            ring_copy(step - 1, way, cut).wait_send()
            cross_copy(step, way, cut).wait_send()
            pair_copy(step, way, cut).wait()
            last_copy(step, way, cut).wait()
        return carry

    lax.fori_loop(1, count, drain, 0)
    for fill in fills:
        fill.wait()
    for cell in range(cells - 2, cells):
        table_copy(cell, cell % 2).wait()


def gather_model(stripe, kernels):
    count = lax.axis_size("sky")
    rows, cols = stripe.shape
    cells = kernels.shape[0]
    cuts = 2
    shape = (count * rows + 2 * ROWPAD, cols + 2 * COLPAD)
    steps = (count - 1, 2, cuts)
    return pl.pallas_call(
        functools.partial(gather_kernel, count, cuts),
        out_shape=[
            jax.ShapeDtypeStruct(shape, stripe.dtype),
            jax.ShapeDtypeStruct((cells, PSF + 1, B, 256), jnp.bfloat16),
        ],
        in_specs=[pl.BlockSpec(memory_space=pl.ANY), pl.BlockSpec(memory_space=pltpu.VMEM)],
        out_specs=[pl.BlockSpec(memory_space=pl.ANY)] * 2,
        scratch_shapes=[
            pltpu.VMEM((shape[0], COLPAD), stripe.dtype),
            pltpu.VMEM((TAPS * 16, 128), jnp.float32),
            pltpu.VMEM((2, PSF + 1, B, 256), jnp.bfloat16),
        ] + [pltpu.SemaphoreType.DMA(steps)] * 8 + [
            pltpu.SemaphoreType.DMA((3 + 2 * (cols // COLPAD),)),
            pltpu.SemaphoreType.DMA((2,)),
        ],
        compiler_params=pltpu.CompilerParams(
            collective_id=0, has_side_effects=True, vmem_limit_bytes=48 * 2**20),
        name="gather_model",
    )(stripe, kernels)


def exchange_kernel(count, data, asked, got, got_asked, data_send, data_recv, id_send, id_recv, local_sem):
    sky = lax.axis_index("sky")
    own = lax.axis_index("exp")
    barrier = pltpu.get_barrier_semaphore()
    for turn in range(1, count):
        pl.semaphore_signal(barrier, inc=1, device_id=((sky + turn) % count, own), device_id_type=MESH)
    pl.semaphore_wait(barrier, count - 1)
    copies = []
    for turn in range(1, count):
        target = (sky + turn) % count
        for source, dest, send, recv in ((data, got, data_send, data_recv), (asked, got_asked, id_send, id_recv)):
            copy = pltpu.make_async_remote_copy(
                src_ref=source.at[target], dst_ref=dest.at[sky],
                send_sem=send.at[turn - 1], recv_sem=recv.at[turn - 1],
                device_id=(target, own), device_id_type=MESH)
            copy.start()
            copies.append(copy)
    for place, (source, dest) in enumerate(((data, got), (asked, got_asked))):
        copy = pltpu.make_async_copy(source.at[sky], dest.at[sky], local_sem.at[place])
        copy.start()
        copies.append(copy)
    for copy in copies:
        copy.wait()


def exchange(data, asked):
    count = lax.axis_size("sky")
    return pl.pallas_call(
        functools.partial(exchange_kernel, count),
        out_shape=[jax.ShapeDtypeStruct(x.shape, x.dtype) for x in (data, asked)],
        in_specs=[pl.BlockSpec(memory_space=pl.ANY)] * 2,
        out_specs=[pl.BlockSpec(memory_space=pl.ANY)] * 2,
        scratch_shapes=[pltpu.SemaphoreType.DMA((count - 1,))] * 4 + [pltpu.SemaphoreType.DMA((2,))],
        compiler_params=pltpu.CompilerParams(
            collective_id=1, has_side_effects=True, vmem_limit_bytes=32 * 2**20),
        name="exchange",
    )(data, asked)


def fold_kernel(stripe_rows, stripe_cols, exps, ids, parts, out, canvas):
    per_row = stripe_cols // B
    canvas[...] = jnp.zeros_like(canvas)
    lane = lax.broadcasted_iota(jnp.int32, (FOLD, B), 1)

    def add(slot, carry):
        block = ids[slot]

        @pl.when(block >= 0)
        def _():
            row0 = pl.multiple_of(block // per_row * B, B)
            col0 = pl.multiple_of(block % per_row * B, B)
            values = parts[slot].astype(jnp.float32)
            canvas[pl.ds(row0, EXT), pl.ds(col0, B)] += values[0:EXT]
            tails = values[EXT:PACKED]
            for third in range(3):
                turned = pltpu.roll(tails, B - 2 * HALO * third, 1) if third else tails
                turned = jnp.where(lane < 2 * HALO, turned, 0.0)
                first = pl.multiple_of(row0 + FOLD * third, 8)
                canvas[pl.ds(first, FOLD), pl.ds(pl.multiple_of(col0 + B, B), B)] += turned

        return carry

    lax.fori_loop(0, ids.shape[0], add, 0)
    width = stripe_cols + B
    middle = pltpu.roll(canvas[...], width - HALO, 1)[:, 0:stripe_cols]
    upper = jnp.concatenate([jnp.zeros((RIM - HALO, stripe_cols), jnp.float32), middle[0:HALO]], 0)
    lower = middle[stripe_rows + HALO : stripe_rows + HALO + RIM]
    rows = jnp.concatenate([middle[HALO : HALO + stripe_rows], upper, lower], 0).astype(out.dtype)
    share = stripe_cols // exps
    for e in range(exps):
        out[e] = rows[:, e * share : (e + 1) * share]


def fold(ids, parts, stripe_rows, stripe_cols, exps):
    shape = (exps, stripe_rows + 2 * RIM, stripe_cols // exps)
    return pl.pallas_call(
        functools.partial(fold_kernel, stripe_rows, stripe_cols, exps),
        grid_spec=pltpu.PrefetchScalarGridSpec(
            num_scalar_prefetch=1,
            grid=(1,),
            in_specs=[pl.BlockSpec(parts.shape, lambda i, ids: (0, 0, 0))],
            out_specs=pl.BlockSpec(shape, lambda i, ids: (0, 0, 0)),
            scratch_shapes=[pltpu.VMEM((stripe_rows + 56, stripe_cols + B), jnp.float32)],
        ),
        out_shape=jax.ShapeDtypeStruct(shape, jnp.bfloat16),
        compiler_params=pltpu.CompilerParams(vmem_limit_bytes=40 * 2**20),
        name="fold",
    )(ids, parts)


def reduce_kernel(skies, exps, parts, out, held, rims, rims_in, send, recv, rim_send, rim_recv):
    sky = lax.axis_index("sky")
    own = lax.axis_index("exp")
    above, below = (sky + skies - 1) % skies, (sky + 1) % skies
    rows = out.shape[0]
    barrier = pltpu.get_barrier_semaphore()
    targets = [(sky, (own + turn) % exps) for turn in range(1, exps)] + [(above, own), (below, own)]
    for target in targets:
        pl.semaphore_signal(barrier, inc=1, device_id=target, device_id_type=MESH)
    pl.semaphore_wait(barrier, len(targets))
    copies = []
    for turn in range(1, exps):
        target = (own + turn) % exps
        copy = pltpu.make_async_remote_copy(
            src_ref=parts.at[target], dst_ref=held.at[turn - 1],
            send_sem=send.at[turn - 1], recv_sem=recv.at[turn - 1],
            device_id=(sky, target), device_id_type=MESH)
        copy.start()
        copies.append(copy)
    for copy in copies:
        copy.wait_recv()

    def total(first, size):
        value = parts[own, first : first + size].astype(jnp.float32)
        for turn in range(1, exps):
            value = value + held[turn - 1, first : first + size].astype(jnp.float32)
        return value

    rims[0] = total(rows, RIM).astype(rims.dtype)
    rims[1] = total(rows + RIM, RIM).astype(rims.dtype)
    for side, target in enumerate((above, below)):
        copy = pltpu.make_async_remote_copy(
            src_ref=rims.at[side], dst_ref=rims_in.at[side],
            send_sem=rim_send.at[side], recv_sem=rim_recv.at[side],
            device_id=(target, own), device_id_type=MESH)
        copy.start()
        copies.append(copy)
    out[RIM : rows - RIM] = total(RIM, rows - 2 * RIM)
    top = total(0, RIM)
    bottom = total(rows - RIM, RIM)
    for copy in copies[-2:]:
        copy.wait_recv()
    has_above = jnp.full(top.shape, sky, jnp.int32) > 0
    has_below = jnp.full(top.shape, sky, jnp.int32) < skies - 1
    out[0:RIM] = top + jnp.where(has_above, rims_in[1].astype(jnp.float32), 0.0)
    out[rows - RIM : rows] = bottom + jnp.where(has_below, rims_in[0].astype(jnp.float32), 0.0)
    for copy in copies:
        copy.wait_send()


def reduce_parts(parts):
    skies, exps = lax.axis_size("sky"), lax.axis_size("exp")
    _, height, share = parts.shape
    rim = (2, RIM, share)
    return pl.pallas_call(
        functools.partial(reduce_kernel, skies, exps),
        out_shape=jax.ShapeDtypeStruct((height - 2 * RIM, share), jnp.float32),
        in_specs=[pl.BlockSpec(memory_space=pltpu.VMEM)],
        out_specs=pl.BlockSpec(memory_space=pltpu.VMEM),
        scratch_shapes=[
            pltpu.VMEM((exps - 1, height, share), parts.dtype),
            pltpu.VMEM(rim, parts.dtype),
            pltpu.VMEM(rim, parts.dtype),
            pltpu.SemaphoreType.DMA((exps - 1,)),
            pltpu.SemaphoreType.DMA((exps - 1,)),
            pltpu.SemaphoreType.DMA((2,)),
            pltpu.SemaphoreType.DMA((2,)),
        ],
        compiler_params=pltpu.CompilerParams(
            collective_id=2, has_side_effects=True, vmem_limit_bytes=32 * 2**20),
        name="reduce_parts",
    )(parts)


def piece_kernel(row_ref, col_ref, cell_ref, slot_ref, whole, bands, observed, keep,
                 residual_out, adjoint_out, windows, patch, rbuf, window_sem):
    piece = pl.program_id(0)
    tt = bands.at[0]

    def fetch(index):
        row0 = pl.multiple_of(row_ref[index], 128)
        col0 = pl.multiple_of(col_ref[index], 128)
        return pltpu.make_async_copy(
            whole.at[pl.ds(row0, 192), pl.ds(col0, 384)], windows.at[index % 2], window_sem.at[index % 2])

    @pl.when(piece == 0)
    def _():
        rbuf[...] = jnp.zeros_like(rbuf)
        fetch(0).start()

    @pl.when(piece + 1 < pl.num_programs(0))
    def _():
        fetch(piece + 1).start()

    fetch(piece).wait()
    window = windows[piece % 2].astype(jnp.float32)
    shifted = window[ROWPAD - HALO : ROWPAD - HALO + AROWS]
    shifted = pltpu.roll(shifted, 384 - (COLPAD - HALO), 1)[:, 0:256]
    patch[...] = shifted.astype(jnp.bfloat16)

    total = None
    for s in range(14, -1, -2):
        acc = None
        for q in range(3):
            a = 16 * q + s
            if a >= PSF:
                continue
            band = tt[a : a + 2].reshape(256, 256)
            term = lax.dot_general(patch[16 * q : 16 * q + 144, :], band,
                                   (((1,), (1,)), ((), ())), preferred_element_type=jnp.float32)
            acc = term if acc is None else acc + term
        if total is None:
            total = acc[:, 128:256]
        else:
            total = pltpu.roll(total, 143, 0) + acc[:, 128:256]
        total = pltpu.roll(total, 143, 0) + acc[:, 0:128]
    predicted = total[0:B]
    residual = (keep[0].astype(jnp.float32) * (predicted - observed[0].astype(jnp.float32)))
    residual = residual.astype(jnp.bfloat16)
    residual_out[0] = residual
    wide = jnp.concatenate([residual.astype(jnp.float32), jnp.zeros((16, B), jnp.float32)], 0)
    rbuf[32 : 32 + B, 0:128] = residual
    rbuf[32 : 32 + B + 16, 128:256] = pltpu.roll(wide, 1, 0).astype(jnp.bfloat16)

    back = None
    for s in range(14, -1, -2):
        acc = None
        for q in range(3):
            a = 16 * q + s
            if a >= PSF:
                continue
            band = tt[a : a + 2].reshape(256, 256)
            term = jnp.dot(rbuf[32 - 16 * q : 32 - 16 * q + AROWS, :], band,
                           preferred_element_type=jnp.float32)
            acc = term if acc is None else acc + term
        back = acc if back is None else pltpu.roll(back, 2, 0) + acc
    tails = back[0:EXT, 128:256]
    packed = tails[0:FOLD]
    for third in range(1, 3):
        packed = packed + pltpu.roll(tails[third * FOLD : (third + 1) * FOLD], 2 * HALO * third, 1)
    adjoint_out[0] = jnp.concatenate([back[0:EXT, 0:128], packed], 0).astype(jnp.bfloat16)


def run_pieces(rows, cols, cells, slots, whole, base, observed, keep, slot_total):
    count = observed.shape[0]
    flops = count * 21 * 2 * 256 * 256 * (144 + AROWS)
    return pl.pallas_call(
        piece_kernel,
        grid_spec=pltpu.PrefetchScalarGridSpec(
            num_scalar_prefetch=4,
            grid=(count,),
            in_specs=[
                pl.BlockSpec(memory_space=pl.ANY),
                pl.BlockSpec((1, PSF + 1, B, 256), lambda p, r, c, k, s: (k[p], 0, 0, 0)),
                pl.BlockSpec((1, B, B), lambda p, r, c, k, s: (p, 0, 0)),
                pl.BlockSpec((1, B, B), lambda p, r, c, k, s: (p, 0, 0)),
            ],
            out_specs=[
                pl.BlockSpec((1, B, B), lambda p, r, c, k, s: (p, 0, 0)),
                pl.BlockSpec((1, PACKED, B), lambda p, r, c, k, s: (s[p], 0, 0)),
            ],
            scratch_shapes=[
                pltpu.VMEM((2, 192, 384), jnp.bfloat16),
                pltpu.VMEM((AROWS, 256), jnp.bfloat16),
                pltpu.VMEM((32 + AROWS, 256), jnp.bfloat16),
                pltpu.SemaphoreType.DMA((2,)),
            ],
        ),
        out_shape=[
            jax.ShapeDtypeStruct((count, B, B), jnp.bfloat16),
            jax.ShapeDtypeStruct((slot_total, PACKED, B), jnp.bfloat16),
        ],
        compiler_params=pltpu.CompilerParams(vmem_limit_bytes=56 * 2**20),
        cost_estimate=pl.CostEstimate(flops=flops, bytes_accessed=16 * 2**20, transcendentals=0),
        name="pieces",
    )(rows, cols, cells, slots, whole, base, observed, keep)


def shards(sky_model, exposure_data, pixel_mask, block_owner, block_local, psf_cell, psf_table):
    sky_count = lax.axis_size("sky")
    exp_count = lax.axis_size("exp")
    stripe_rows, stripe_cols = sky_model.shape
    per_row = stripe_cols // B
    block_rows = stripe_rows // B
    piece_count = exposure_data.shape[0]
    slot_total = sky_count * CAP
    owner_sky = block_owner[:, 0]
    index = lax.broadcasted_iota(jnp.int32, (piece_count, piece_count), 0)
    earlier = lax.broadcasted_iota(jnp.int32, (piece_count, piece_count), 1) < index
    same_owner = owner_sky[:, None] == owner_sky[None, :]
    rank_within = jnp.sum((same_owner & earlier).astype(jnp.int32), axis=1)
    slot_index = owner_sky * CAP + rank_within
    named = slot_index[None, :] == lax.broadcasted_iota(jnp.int32, (slot_total, piece_count), 0)
    requests = jnp.sum(jnp.where(named, block_local[None, :] + 1, 0), axis=1) - 1
    requests = requests.reshape(sky_count, 1, CAP)
    requests = jnp.pad(requests, ((0, 0), (0, 7), (0, 128 - CAP)))
    cell_count = psf_table.shape[0]
    kernels = psf_table.reshape(cell_count, PSF, PSF)
    kernels = jnp.pad(kernels, ((0, 0), (0, TAPS - PSF), (0, 128 - PSF)))

    whole, table = gather_model(sky_model, kernels)
    row_start = (owner_sky * block_rows + block_local // per_row) * B
    col_start = block_local % per_row * B
    residuals, adjoints = run_pieces(
        row_start, col_start, psf_cell, slot_index, whole, table, exposure_data, pixel_mask, slot_total
    )
    received, asked = exchange(adjoints.reshape(sky_count, CAP, PACKED, B), requests)
    ids = asked[:, 0, :CAP].reshape(slot_total)
    parts = fold(ids, received.reshape(slot_total, PACKED, B), stripe_rows, stripe_cols, exp_count)
    return (reduce_parts(parts), residuals)


def solution(mesh):
    in_specs = (
        P("sky", None),
        P(("sky", "exp"), None, None),
        P(("sky", "exp"), None, None),
        P(("sky", "exp"), None),
        P(("sky", "exp")),
        P(("sky", "exp")),
        P("exp", None),
    )
    out_specs = (P("sky", "exp"), P(("sky", "exp"), None, None))
    return jax.shard_map(shards, mesh=mesh, in_specs=in_specs, out_specs=out_specs, check_vma=False)
```

```python
import functools

import jax
import jax.numpy as jnp
from jax import lax
from jax.experimental import pallas as pl
from jax.experimental.pallas import tpu as pltpu
from jax.sharding import PartitionSpec as P

B = 128
PSF = 41
HALO = 20
CAP = 2
EXT = B + 2 * HALO
TAPS = 48
ROWPAD = 32
COLPAD = 128
AROWS = 176


MESH = pl.DeviceIdType.MESH
PACKED = 224
FOLD = 56
RIM = 32


def ring_place(sky, count):
    odd = sky % 2
    return (sky // 2) * (1 - odd) + (count - 1 - sky // 2) * odd


def ring_sky(place, count):
    late = place // (count // 2)
    return 2 * place * (1 - late) + (2 * (count - 1 - place) + 1) * late


def gather_kernel(count, cuts, stripe, kernels, whole, table, zero, spaced, bands, ring_send, ring_recv,
                  pair_send, pair_recv, cross_send, cross_recv, last_send, last_recv, local_sem, table_sem):
    sky = lax.axis_index("sky")
    own = lax.axis_index("exp")
    core = own % 2
    half = (own % 4) // 2
    pair = own + 1 - 2 * core
    cross = own + 2 - 4 * half
    place = ring_place(sky, count)
    ahead = ring_sky((place + 1) % count, count)
    behind = ring_sky((place + count - 1) % count, count)
    rows, cols = stripe.shape
    cells = kernels.shape[0]
    part = rows // (8 * cuts)
    quarter, other = core + 2 * half, core + 2 * (1 - half)

    barrier = pltpu.get_barrier_semaphore()
    for target in ((ahead, own), (behind, own), (sky, pair), (sky, cross)):
        pl.semaphore_signal(barrier, inc=1, device_id=target, device_id_type=MESH)
    pl.semaphore_wait(barrier, 4)

    def inner(share, way, cut):
        return share * (rows // 4) + way * (rows // 8) + cut * part

    def spot(share, step, way, cut):
        origin = ring_sky((place + count - (1 - 2 * way) * step) % count, count)
        first = pl.multiple_of(ROWPAD + origin * rows + inner(share, way, cut), 16)
        return whole.at[pl.ds(first, part), pl.ds(COLPAD, cols)]

    def ring_copy(step, way, cut, first=False):
        dest = spot(quarter, step, way, cut)
        source = stripe.at[pl.ds(pl.multiple_of(inner(quarter, way, cut), 16), part), :] if first else dest
        return pltpu.make_async_remote_copy(
            src_ref=source, dst_ref=dest,
            send_sem=ring_send.at[step, way, cut], recv_sem=ring_recv.at[step, way, cut],
            device_id=((behind if way else ahead), own), device_id_type=MESH)

    def hand_on(share, step, way, cut, send, recv, target):
        block = spot(share, step, way, cut)
        return pltpu.make_async_remote_copy(
            src_ref=block, dst_ref=block, send_sem=send.at[step - 1, way, cut],
            recv_sem=recv.at[step - 1, way, cut], device_id=(sky, target), device_id_type=MESH)

    def pair_copy(step, way, cut):
        return hand_on(quarter, step, way, cut, pair_send, pair_recv, pair)

    def cross_copy(step, way, cut):
        return hand_on(quarter, step, way, cut, cross_send, cross_recv, cross)

    def last_copy(step, way, cut):
        return hand_on(other, step, way, cut, last_send, last_recv, pair)

    each = [(cut, way) for cut in range(cuts) for way in range(2)]
    for cut, way in each:
        ring_copy(0, way, cut, True).start()

    zero[...] = jnp.zeros_like(zero)
    total = whole.shape[0]
    fills = []
    mine = pl.multiple_of(ROWPAD + sky * rows, 16)
    fills.append(pltpu.make_async_copy(stripe, whole.at[pl.ds(mine, rows), pl.ds(COLPAD, cols)], local_sem.at[0]))
    for side in range(2):
        fills.append(pltpu.make_async_copy(
            zero, whole.at[:, pl.ds(side * (COLPAD + cols), COLPAD)], local_sem.at[1 + side]))
    for side in range(2):
        for block in range(cols // COLPAD):
            fills.append(pltpu.make_async_copy(
                zero.at[pl.ds(0, ROWPAD), :],
                whole.at[pl.ds(side * (total - ROWPAD), ROWPAD), pl.ds(COLPAD * (1 + block), COLPAD)],
                local_sem.at[3 + side * (cols // COLPAD) + block]))
    for fill in fills:
        fill.start()

    def table_copy(cell, slot):
        return pltpu.make_async_copy(bands.at[slot], table.at[cell], table_sem.at[slot])

    def build(cell):
        slot = cell % 2

        @pl.when(cell >= 2)
        def _():
            table_copy(cell, slot).wait()

        kernel = kernels[cell].astype(jnp.float32)
        for j in range(16):
            spaced[pl.ds(j, TAPS, stride=16), :] = pltpu.roll(kernel, j, 1) if j else kernel
        bands[slot] = spaced[0 : PSF * 16].astype(jnp.bfloat16)
        table_copy(cell, slot).start()

    early = max(0, cells - (count - 1) * cuts)

    def build_early(cell, carry):
        build(cell)
        return carry

    lax.fori_loop(0, early, build_early, 0)

    def ring_step(step, carry):
        for cut in range(cuts):
            for way in range(2):
                ring_copy(step - 1, way, cut).wait_recv()

                @pl.when(step < count - 1)
                def _():
                    ring_copy(step, way, cut).start()

                cross_copy(step, way, cut).start()
                pair_copy(step, way, cut).start()

                @pl.when(step > 1)
                def _():
                    cross_copy(step - 1, way, cut).wait_recv()
                    last_copy(step - 1, way, cut).start()

            cell = early + (step - 1) * cuts + cut

            @pl.when(cell < cells)
            def _():
                build(cell)

        return carry

    lax.fori_loop(1, count, ring_step, 0)
    for cut, way in each:
        cross_copy(count - 1, way, cut).wait_recv()
        last_copy(count - 1, way, cut).start()

    def drain(step, carry):
        for cut, way in each:
            ring_copy(step - 1, way, cut).wait_send()
            cross_copy(step, way, cut).wait_send()
            pair_copy(step, way, cut).wait()
            last_copy(step, way, cut).wait()
        return carry

    lax.fori_loop(1, count, drain, 0)
    for fill in fills:
        fill.wait()
    for cell in range(cells - 2, cells):
        table_copy(cell, cell % 2).wait()


def gather_model(stripe, kernels):
    count = lax.axis_size("sky")
    rows, cols = stripe.shape
    cells = kernels.shape[0]
    cuts = 2
    shape = (count * rows + 2 * ROWPAD, cols + 2 * COLPAD)
    steps = (count - 1, 2, cuts)
    return pl.pallas_call(
        functools.partial(gather_kernel, count, cuts),
        out_shape=[
            jax.ShapeDtypeStruct(shape, stripe.dtype),
            jax.ShapeDtypeStruct((cells, PSF * 16, 128), jnp.bfloat16),
        ],
        in_specs=[pl.BlockSpec(memory_space=pl.ANY), pl.BlockSpec(memory_space=pltpu.VMEM)],
        out_specs=[pl.BlockSpec(memory_space=pl.ANY)] * 2,
        scratch_shapes=[
            pltpu.VMEM((shape[0], COLPAD), stripe.dtype),
            pltpu.VMEM((TAPS * 16, 128), jnp.float32),
            pltpu.VMEM((2, PSF * 16, 128), jnp.bfloat16),
        ] + [pltpu.SemaphoreType.DMA(steps)] * 8 + [
            pltpu.SemaphoreType.DMA((3 + 2 * (cols // COLPAD),)),
            pltpu.SemaphoreType.DMA((2,)),
        ],
        compiler_params=pltpu.CompilerParams(
            collective_id=0, has_side_effects=True, vmem_limit_bytes=48 * 2**20),
        name="gather_model",
    )(stripe, kernels)


def fold_kernel(stripe_rows, stripe_cols, exps, ids, slots, parts, by_slot, out, residual_out, canvas):
    per_row = stripe_cols // B
    canvas[...] = jnp.zeros_like(canvas)
    lane = lax.broadcasted_iota(jnp.int32, (FOLD, B), 1)

    def add(slot, carry):
        block = ids[slot]

        @pl.when(block >= 0)
        def _():
            row0 = pl.multiple_of(block // per_row * B, B)
            col0 = pl.multiple_of(block % per_row * B, B)
            values = parts[slot].astype(jnp.float32)
            canvas[pl.ds(row0, EXT), pl.ds(col0, B)] += values[0:EXT]
            tails = values[EXT:PACKED]
            for third in range(3):
                turned = pltpu.roll(tails, B - 2 * HALO * third, 1) if third else tails
                turned = jnp.where(lane < 2 * HALO, turned, 0.0)
                first = pl.multiple_of(row0 + FOLD * third, 8)
                canvas[pl.ds(first, FOLD), pl.ds(pl.multiple_of(col0 + B, B), B)] += turned

        return carry

    lax.fori_loop(0, ids.shape[0], add, 0)

    def reorder(piece, carry):
        residual_out[piece] = by_slot[slots[piece]]
        return carry

    lax.fori_loop(0, slots.shape[0], reorder, 0)
    width = stripe_cols + B
    middle = pltpu.roll(canvas[...], width - HALO, 1)[:, 0:stripe_cols]
    upper = jnp.concatenate([jnp.zeros((RIM - HALO, stripe_cols), jnp.float32), middle[0:HALO]], 0)
    lower = middle[stripe_rows + HALO : stripe_rows + HALO + RIM]
    rows = jnp.concatenate([middle[HALO : HALO + stripe_rows], upper, lower], 0).astype(out.dtype)
    share = stripe_cols // exps
    for e in range(exps):
        out[e] = rows[:, e * share : (e + 1) * share]


def fold(ids, slots, parts, by_slot, stripe_rows, stripe_cols, exps):
    shape = (exps, stripe_rows + 2 * RIM, stripe_cols // exps)
    residual_shape = (slots.shape[0], B, B)
    return pl.pallas_call(
        functools.partial(fold_kernel, stripe_rows, stripe_cols, exps),
        grid_spec=pltpu.PrefetchScalarGridSpec(
            num_scalar_prefetch=2,
            grid=(1,),
            in_specs=[
                pl.BlockSpec(parts.shape, lambda i, ids, slots: (0, 0, 0)),
                pl.BlockSpec(by_slot.shape, lambda i, ids, slots: (0, 0, 0)),
            ],
            out_specs=[
                pl.BlockSpec(shape, lambda i, ids, slots: (0, 0, 0)),
                pl.BlockSpec(residual_shape, lambda i, ids, slots: (0, 0, 0)),
            ],
            scratch_shapes=[pltpu.VMEM((stripe_rows + 56, stripe_cols + B), jnp.float32)],
        ),
        out_shape=[
            jax.ShapeDtypeStruct(shape, jnp.bfloat16),
            jax.ShapeDtypeStruct(residual_shape, jnp.bfloat16),
        ],
        compiler_params=pltpu.CompilerParams(vmem_limit_bytes=40 * 2**20),
        name="fold",
    )(ids, slots, parts, by_slot)


def reduce_kernel(skies, exps, parts, out, held, rims, rims_in, send, recv, rim_send, rim_recv):
    sky = lax.axis_index("sky")
    own = lax.axis_index("exp")
    above, below = (sky + skies - 1) % skies, (sky + 1) % skies
    rows = out.shape[0]
    barrier = pltpu.get_barrier_semaphore()
    targets = [(sky, (own + turn) % exps) for turn in range(1, exps)] + [(above, own), (below, own)]
    for target in targets:
        pl.semaphore_signal(barrier, inc=1, device_id=target, device_id_type=MESH)
    pl.semaphore_wait(barrier, len(targets))
    copies = []
    for turn in range(1, exps):
        target = (own + turn) % exps
        copy = pltpu.make_async_remote_copy(
            src_ref=parts.at[target], dst_ref=held.at[turn - 1],
            send_sem=send.at[turn - 1], recv_sem=recv.at[turn - 1],
            device_id=(sky, target), device_id_type=MESH)
        copy.start()
        copies.append(copy)
    for copy in copies:
        copy.wait_recv()

    def total(first, size):
        value = parts[own, first : first + size].astype(jnp.float32)
        for turn in range(1, exps):
            value = value + held[turn - 1, first : first + size].astype(jnp.float32)
        return value

    rims[0] = total(rows, RIM).astype(rims.dtype)
    rims[1] = total(rows + RIM, RIM).astype(rims.dtype)
    for side, target in enumerate((above, below)):
        copy = pltpu.make_async_remote_copy(
            src_ref=rims.at[side], dst_ref=rims_in.at[side],
            send_sem=rim_send.at[side], recv_sem=rim_recv.at[side],
            device_id=(target, own), device_id_type=MESH)
        copy.start()
        copies.append(copy)
    out[RIM : rows - RIM] = total(RIM, rows - 2 * RIM)
    top = total(0, RIM)
    bottom = total(rows - RIM, RIM)
    for copy in copies[-2:]:
        copy.wait_recv()
    has_above = jnp.full(top.shape, sky, jnp.int32) > 0
    has_below = jnp.full(top.shape, sky, jnp.int32) < skies - 1
    out[0:RIM] = top + jnp.where(has_above, rims_in[1].astype(jnp.float32), 0.0)
    out[rows - RIM : rows] = bottom + jnp.where(has_below, rims_in[0].astype(jnp.float32), 0.0)
    for copy in copies:
        copy.wait_send()


def reduce_parts(parts):
    skies, exps = lax.axis_size("sky"), lax.axis_size("exp")
    _, height, share = parts.shape
    rim = (2, RIM, share)
    return pl.pallas_call(
        functools.partial(reduce_kernel, skies, exps),
        out_shape=jax.ShapeDtypeStruct((height - 2 * RIM, share), jnp.float32),
        in_specs=[pl.BlockSpec(memory_space=pltpu.VMEM)],
        out_specs=pl.BlockSpec(memory_space=pltpu.VMEM),
        scratch_shapes=[
            pltpu.VMEM((exps - 1, height, share), parts.dtype),
            pltpu.VMEM(rim, parts.dtype),
            pltpu.VMEM(rim, parts.dtype),
            pltpu.SemaphoreType.DMA((exps - 1,)),
            pltpu.SemaphoreType.DMA((exps - 1,)),
            pltpu.SemaphoreType.DMA((2,)),
            pltpu.SemaphoreType.DMA((2,)),
        ],
        compiler_params=pltpu.CompilerParams(
            collective_id=2, has_side_effects=True, vmem_limit_bytes=32 * 2**20),
        name="reduce_parts",
    )(parts)


def piece_kernel(count, asked, patches, base, observed, keep,
                 residual_out, got, got_asked, outbox, tt, rbuf,
                 data_send, data_recv, id_send, id_recv, local_sem):
    sky = lax.axis_index("sky")
    own = lax.axis_index("exp")
    barrier = pltpu.get_barrier_semaphore()
    for turn in range(1, count):
        pl.semaphore_signal(barrier, inc=1, device_id=((sky + turn) % count, own), device_id_type=MESH)
    pl.semaphore_wait(barrier, count - 1)
    copies = []
    for turn in range(1, count):
        target = (sky + turn) % count
        copies.append(pltpu.make_async_remote_copy(
            src_ref=asked.at[target], dst_ref=got_asked.at[sky],
            send_sem=id_send.at[turn - 1], recv_sem=id_recv.at[turn - 1],
            device_id=(target, own), device_id_type=MESH))
    copies.append(pltpu.make_async_copy(asked.at[sky], got_asked.at[sky], local_sem.at[CAP]))
    for copy in copies:
        copy.start()

    def place_of(turn):
        return ((sky + 1 + turn // CAP) % count) * CAP + turn % CAP

    def send(turn):
        return pltpu.make_async_remote_copy(
            src_ref=outbox.at[place_of(turn)], dst_ref=got.at[sky * CAP + turn % CAP],
            send_sem=data_send.at[turn], recv_sem=data_recv.at[turn],
            device_id=((sky + 1 + turn // CAP) % count, own), device_id_type=MESH)

    tt[...] = jnp.zeros_like(tt)
    rbuf[...] = jnp.zeros_like(rbuf)
    remote = (count - 1) * CAP

    def work(turn, carry):
        slot = place_of(turn)
        patch = patches.at[slot]
        lane = lax.broadcasted_iota(jnp.int32, (PSF, 16, 128), 2)
        taps = base[slot].astype(jnp.float32).reshape(PSF, 16, 128)
        for step in range(B // 16):
            first = 16 * step
            turned = pltpu.roll(taps, first, 2) if first else taps
            over = first + 56 - 128
            if over > 0:
                low = jnp.where(lane >= first, turned, 0.0)
                high = jnp.where(lane < over, turned, 0.0)
                tt[0:PSF, first : first + 16, 128:256] = high.astype(jnp.bfloat16)
            else:
                low = turned
            tt[0:PSF, first : first + 16, 0:128] = low.astype(jnp.bfloat16)
        total = None
        for s in range(14, -1, -2):
            acc = None
            for q in range(3):
                a = 16 * q + s
                if a >= PSF:
                    continue
                band = tt[a : a + 2].reshape(256, 256)
                term = lax.dot_general(patch[16 * q : 16 * q + 144, :], band,
                                       (((1,), (1,)), ((), ())), preferred_element_type=jnp.float32)
                acc = term if acc is None else acc + term
            if total is None:
                total = acc[:, 128:256]
            else:
                total = pltpu.roll(total, 143, 0) + acc[:, 128:256]
            total = pltpu.roll(total, 143, 0) + acc[:, 0:128]
        predicted = total[0:B]
        residual = (keep[slot].astype(jnp.float32) * (predicted - observed[slot].astype(jnp.float32)))
        residual = residual.astype(jnp.bfloat16)
        residual_out[slot] = residual
        wide = jnp.concatenate([residual.astype(jnp.float32), jnp.zeros((16, B), jnp.float32)], 0)
        rbuf[32 : 32 + B, 0:128] = residual
        rbuf[32 : 32 + B + 16, 128:256] = pltpu.roll(wide, 1, 0).astype(jnp.bfloat16)

        back = None
        for s in range(14, -1, -2):
            acc = None
            for q in range(3):
                a = 16 * q + s
                if a >= PSF:
                    continue
                band = tt[a : a + 2].reshape(256, 256)
                term = jnp.dot(rbuf[32 - 16 * q : 32 - 16 * q + AROWS, :], band,
                               preferred_element_type=jnp.float32)
                acc = term if acc is None else acc + term
            back = acc if back is None else pltpu.roll(back, 2, 0) + acc
        tails = back[0:EXT, 128:256]
        packed = tails[0:FOLD]
        for third in range(1, 3):
            packed = packed + pltpu.roll(tails[third * FOLD : (third + 1) * FOLD], 2 * HALO * third, 1)
        outbox[slot] = jnp.concatenate([back[0:EXT, 0:128], packed], 0).astype(jnp.bfloat16)

        @pl.when(turn < remote)
        def _():
            send(turn).start()

        return carry

    lax.fori_loop(0, count * CAP, work, 0)
    for turn in range(CAP):
        copies.append(pltpu.make_async_copy(
            outbox.at[sky * CAP + turn], got.at[sky * CAP + turn], local_sem.at[turn]))
        copies[-1].start()

    def drain(turn, carry):
        send(turn).wait()
        return carry

    lax.fori_loop(0, remote, drain, 0)
    for copy in copies:
        copy.wait()


def run_pieces(asked, whole, base, observed, keep):
    count = lax.axis_size("sky")
    slots = count * CAP
    vmem = pl.BlockSpec(memory_space=pltpu.VMEM)
    hbm = pl.BlockSpec(memory_space=pl.ANY)
    remote = (count - 1) * CAP
    return pl.pallas_call(
        functools.partial(piece_kernel, count),
        out_shape=[
            jax.ShapeDtypeStruct((slots, B, B), jnp.bfloat16),
            jax.ShapeDtypeStruct((slots, PACKED, B), jnp.bfloat16),
            jax.ShapeDtypeStruct(asked.shape, asked.dtype),
        ],
        in_specs=[hbm] + [vmem] * 4,
        out_specs=[vmem, hbm, hbm],
        scratch_shapes=[
            pltpu.VMEM((slots, PACKED, B), jnp.bfloat16),
            pltpu.VMEM((TAPS, B, 256), jnp.bfloat16),
            pltpu.VMEM((32 + AROWS, 256), jnp.bfloat16),
            pltpu.SemaphoreType.DMA((remote,)),
            pltpu.SemaphoreType.DMA((remote,)),
            pltpu.SemaphoreType.DMA((count - 1,)),
            pltpu.SemaphoreType.DMA((count - 1,)),
            pltpu.SemaphoreType.DMA((CAP + 1,)),
        ],
        compiler_params=pltpu.CompilerParams(
            collective_id=1, has_side_effects=True, vmem_limit_bytes=48 * 2**20),
        name="pieces",
    )(asked, whole, base, observed, keep)


def arrange_kernel(rows, cols, cells, order, whole, base, observed, keep,
                   patch_out, base_out, observed_out, keep_out):
    slot = pl.program_id(0)
    row0 = pl.multiple_of(rows[slot], 128)
    col0 = pl.multiple_of(cols[slot], 128)
    window = whole[pl.ds(row0, 192), pl.ds(col0, 384)].astype(jnp.float32)
    shifted = window[ROWPAD - HALO : ROWPAD - HALO + AROWS]
    shifted = pltpu.roll(shifted, 384 - (COLPAD - HALO), 1)[:, 0:256]
    patch_out[0] = shifted.astype(jnp.bfloat16)
    base_out[...] = base[...]
    observed_out[...] = observed[...]
    keep_out[...] = keep[...].astype(jnp.float32).astype(jnp.bfloat16)


def arrange(rows, cols, cells, order, whole, base, observed, keep):
    slots = rows.shape[0]
    shapes = [(AROWS, 256), (PSF * 16, 128), (B, B), (B, B)]

    def by_order(i, r, c, k, o):
        return (o[i], 0, 0)

    return pl.pallas_call(
        arrange_kernel,
        grid_spec=pltpu.PrefetchScalarGridSpec(
            num_scalar_prefetch=4,
            grid=(slots,),
            in_specs=[
                pl.BlockSpec(whole.shape, lambda i, r, c, k, o: (0, 0)),
                pl.BlockSpec((1, PSF * 16, 128), lambda i, r, c, k, o: (k[i], 0, 0)),
                pl.BlockSpec((1, B, B), by_order),
                pl.BlockSpec((1, B, B), by_order),
            ],
            out_specs=[pl.BlockSpec((1,) + s, lambda i, r, c, k, o: (i, 0, 0)) for s in shapes],
        ),
        out_shape=[jax.ShapeDtypeStruct((slots,) + s, jnp.bfloat16) for s in shapes],
        compiler_params=pltpu.CompilerParams(vmem_limit_bytes=40 * 2**20),
        name="arrange",
    )(rows, cols, cells, order, whole, base, observed, keep)


def shards(sky_model, exposure_data, pixel_mask, block_owner, block_local, psf_cell, psf_table):
    sky_count = lax.axis_size("sky")
    exp_count = lax.axis_size("exp")
    stripe_rows, stripe_cols = sky_model.shape
    per_row = stripe_cols // B
    block_rows = stripe_rows // B
    piece_count = exposure_data.shape[0]
    slot_total = sky_count * CAP
    owner_sky = block_owner[:, 0]
    index = lax.broadcasted_iota(jnp.int32, (piece_count, piece_count), 0)
    earlier = lax.broadcasted_iota(jnp.int32, (piece_count, piece_count), 1) < index
    same_owner = owner_sky[:, None] == owner_sky[None, :]
    rank_within = jnp.sum((same_owner & earlier).astype(jnp.int32), axis=1)
    slot_index = owner_sky * CAP + rank_within
    named = slot_index[None, :] == lax.broadcasted_iota(jnp.int32, (slot_total, piece_count), 0)
    requests = jnp.sum(jnp.where(named, block_local[None, :] + 1, 0), axis=1) - 1
    requests = requests.reshape(sky_count, 1, CAP)
    requests = jnp.pad(requests, ((0, 0), (0, 7), (0, 128 - CAP)))
    cell_count = psf_table.shape[0]
    kernels = psf_table.reshape(cell_count, PSF, PSF)
    kernels = jnp.pad(kernels, ((0, 0), (0, TAPS - PSF), (0, 128 - PSF)))

    whole, table = gather_model(sky_model, kernels)
    row_start = (owner_sky * block_rows + block_local // per_row) * B
    col_start = block_local % per_row * B
    order = jnp.sum(jnp.where(named, jnp.arange(piece_count, dtype=jnp.int32)[None, :], 0), axis=1)

    def by_slot(values):
        return jnp.sum(jnp.where(named, values[None, :], 0), axis=1)

    arranged = arrange(
        by_slot(row_start), by_slot(col_start), by_slot(psf_cell), order, whole, table,
        exposure_data, pixel_mask,
    )
    residuals, received, asked = run_pieces(requests, *arranged)
    ids = asked[:, 0, :CAP].reshape(slot_total)
    parts, residuals = fold(ids, slot_index, received, residuals, stripe_rows, stripe_cols, exp_count)
    return (reduce_parts(parts), residuals)


def solution(mesh):
    in_specs = (
        P("sky", None),
        P(("sky", "exp"), None, None),
        P(("sky", "exp"), None, None),
        P(("sky", "exp"), None),
        P(("sky", "exp")),
        P(("sky", "exp")),
        P("exp", None),
    )
    out_specs = (P("sky", "exp"), P(("sky", "exp"), None, None))
    return jax.shard_map(shards, mesh=mesh, in_specs=in_specs, out_specs=out_specs, check_vma=False)
```
